128 devices in a mesh: replica: 8 (over y_lo, x), tensor: 16 (over y_hi, z, core).
Axes of the slice: x: 4, y: 4 (y_hi: 2, y_lo: 2; y = y_hi * 2 + y_lo), z: 4, core: 2. Of those that a mesh axis runs over, the one named last changes fastest.
Arguments:
- tokens: bfloat16 [2048, 4096], P(('replica', 'tensor')), may hold values from -6 to 6
- cotangent: bfloat16 [2048, 4096], P(('replica', 'tensor')), may hold values from -6 to 6
- w_gate: bfloat16 [4096, 14336], P(None, 'tensor'), may hold values from -0.09375 to 0.09375
- w_up: bfloat16 [4096, 14336], P(None, 'tensor'), may hold values from -0.09375 to 0.09375
- w_down: bfloat16 [14336, 4096], P('tensor'), may hold values from -0.046875 to 0.046875
- outer_frag: float32 [512, 4096], P('tensor'), may hold values from -6 to 6
- local_frag: bfloat16 [8, 512, 4096], P('replica', 'tensor'), may hold values from -6 to 6
- momentum: float32 [512, 4096], P('tensor'), may hold values from -4 to 4
Outputs:
- layer_output: float32 [2048, 4096], P(('replica', 'tensor'))
- input_grad: float32 [2048, 4096], P(('replica', 'tensor'))
- new_outer: float32 [512, 4096], P('tensor')
- new_momentum: float32 [512, 4096], P('tensor')
The draws below stay inside these ranges and needn't reach their ends.
All inputs are finite; a program needn't handle non-finite values.
Results may differ from the reference program's by a relative error of at most 0.0029.
Values may be sent and summed in bfloat16 or wider, within the bound.
No kernel may reach another device: no remote copies, remote signals or barrier semaphores. Data moves between devices by JAX's collectives and lax.ppermute only.
A program may use at most 128 MiB of HBM per device.

```python
import jax
import jax.numpy as jnp

D = 4096
FF = 14336
TOKENS = 2048
FRAG = 512
N_REPLICA = 8


def levels(stream_key, extent, split, smallest, high):
    level, own = 1.0, jax.random.fold_in(stream_key, 6)
    for axis_at, shards_of in split:
        heights = jnp.exp(jax.random.uniform(jax.random.fold_in(own, axis_at), (shards_of,), jnp.float32, smallest / len(split), high / len(split)))
        level = level * jnp.repeat(heights, extent[axis_at] // shards_of).reshape([-1 if axis == axis_at else 1 for axis in range(len(extent))])
    return level


def centred(stream_key, dims, scale, reach, shards=(), held_as=jnp.bfloat16):
    result = jax.random.normal(stream_key, dims, jnp.float32) * scale
    if len(shards) > 0:
        result = levels(stream_key, dims, shards, -0.22, 0.18) * result
    return jnp.clip(result, min=-reach, max=reach).astype(held_as)


def setup_inputs(seed: int = 0) -> dict:
    seeds = jax.random.split(jax.random.key(seed), 9)
    tokens = centred(seeds[0], (TOKENS, D), 1.0, 6.0, ((0, 128),))
    cotangent = centred(seeds[1], (TOKENS, D), 1.0, 6.0, ((0, 128),))
    w_gate = centred(seeds[2], (D, FF), D ** -0.5, 0.09375, ((1, 16),))
    w_up = centred(seeds[3], (D, FF), D ** -0.5, 0.09375, ((1, 16),))
    w_down = centred(seeds[4], (FF, D), FF ** -0.5, 0.046875, ((0, 16),))
    outer_frag = centred(seeds[5], (FRAG, D), 1.0, 6.0, ((0, 16),), jnp.float32)
    local_frag = centred(seeds[6], (N_REPLICA, FRAG, D), 1.0, 6.0, ((0, 8), (1, 16)))
    momentum = centred(seeds[7], (FRAG, D), 0.5, 4.0, ((0, 16),), jnp.float32)
    return {"tokens": tokens, "cotangent": cotangent, "w_gate": w_gate, "w_up": w_up, "w_down": w_down, "outer_frag": outer_frag, "local_frag": local_frag, "momentum": momentum}


outer_rate = 0.7
outer_beta = 0.9


def reference(tokens, cotangent, w_gate, w_up, w_down, outer_frag, local_frag, momentum):
    pre_gate = jnp.dot(tokens, w_gate, preferred_element_type=jnp.float32)
    pre_up = jnp.dot(tokens, w_up, preferred_element_type=jnp.float32)
    sigmoid_gate = jax.nn.sigmoid(pre_gate)
    hidden = (pre_gate * sigmoid_gate * pre_up).astype(jnp.bfloat16)
    layer_output = jnp.dot(hidden, w_down, preferred_element_type=jnp.float32)
    d_hidden = jnp.dot(cotangent, w_down.T, preferred_element_type=jnp.float32)
    d_gate = (d_hidden * pre_up * sigmoid_gate * (1.0 + pre_gate * (1.0 - sigmoid_gate))).astype(jnp.bfloat16)
    d_up = (d_hidden * pre_gate * sigmoid_gate).astype(jnp.bfloat16)
    input_grad = (jnp.dot(d_gate, w_gate.T, preferred_element_type=jnp.float32)
                  + jnp.dot(d_up, w_up.T, preferred_element_type=jnp.float32))
    pseudo = jnp.sum(outer_frag[None] - local_frag.astype(jnp.float32), axis=0)
    mean_delta = pseudo / N_REPLICA
    new_momentum = outer_beta * momentum + mean_delta
    new_outer = outer_frag - outer_rate * (mean_delta + outer_beta * new_momentum)
    return layer_output, input_grad, new_outer, new_momentum
```

```python
import jax
import jax.numpy as jnp
from jax import lax
from jax.sharding import PartitionSpec as P

outer_rate = 0.7
outer_beta = 0.9
AXES = ("replica", "tensor")
EXTENT_X, EXTENT_Y, EXTENT_Z = 4, 4, 4


def position(x, y, z, core):
    return ((y % 2) * EXTENT_X + x) * 16 + (y // 2) * 8 + z * 2 + core


def pairs(move):
    return [
        (position(x, y, z, core), position(*move(x, y, z, core)))
        for x in range(EXTENT_X)
        for y in range(EXTENT_Y)
        for z in range(EXTENT_Z)
        for core in range(2)
    ]


def send_z(rows, distance):
    return lax.ppermute(
        rows, AXES, pairs(lambda x, y, z, core: (x, y, (z + distance) % EXTENT_Z, core))
    )


def swap_y(rows):
    return lax.ppermute(rows, AXES, pairs(lambda x, y, z, core: (x, 3 - y, z, core)))


def swap_core(rows):
    return lax.ppermute(rows, AXES, pairs(lambda x, y, z, core: (x, y, z, 1 - core)))


def times_transpose(left_rows, weight):
    return lax.dot_general(
        left_rows, weight, (((1,), (1,)), ((), ())), preferred_element_type=jnp.float32
    )


def gather_y_first(rows):
    both = jnp.concatenate([rows, swap_y(rows)], 0)
    near = jnp.concatenate([both] + order_z(both), 0)
    return jnp.concatenate([near, swap_core(near)], 0)


def order_z(block):
    one, three, two = send_z(block, -1), send_z(block, -3), send_z(block, -2)
    return [one, two, three]


def gather_z_first(rows):
    line = jnp.concatenate([rows] + order_z(rows), 0)
    across = swap_y(line)
    width = rows.shape[1]
    near = jnp.stack([line.reshape(4, 16, width), across.reshape(4, 16, width)], 1)
    near = near.reshape(128, width)
    return jnp.concatenate([near, swap_core(near)], 0)


def half(rows):
    return rows.astype(jnp.bfloat16)


def full(rows):
    return rows.astype(jnp.float32)


def sum_cores(partial):
    return partial[:128] + full(swap_core(half(partial[128:])))


def scatter_z_first(partial):
    blocks = sum_cores(partial).reshape(4, 32, -1)
    sent = half(blocks[1:])
    arrived = [send_z(sent[d - 1], d) for d in (1, 3, 2)]
    both = blocks[0] + full(arrived[0]) + full(arrived[1]) + full(arrived[2])
    return both[:16] + full(swap_y(half(both[16:])))


def scatter_y_first(partial):
    blocks = sum_cores(partial).reshape(4, 2, 16, -1)
    line = blocks[:, 0] + full(swap_y(half(blocks[:, 1])))
    sent = half(line[1:])
    arrived = [send_z(sent[d - 1], d) for d in (1, 3, 2)]
    return line[0] + full(arrived[0]) + full(arrived[1]) + full(arrived[2])


def on_device(tokens, cotangent, w_gate, w_up, w_down, outer_frag, local_frag, momentum):
    every_local = lax.all_gather(local_frag[0], "replica", axis=0, tiled=False)
    token_rows = gather_y_first(tokens)
    cotangent_rows = gather_z_first(cotangent)
    pre_gate = jnp.dot(token_rows, w_gate, preferred_element_type=jnp.float32)
    pre_up = jnp.dot(token_rows, w_up, preferred_element_type=jnp.float32)
    sigmoid_gate = jax.nn.sigmoid(pre_gate)
    hidden = (pre_gate * sigmoid_gate * pre_up).astype(jnp.bfloat16)
    layer_output = scatter_z_first(jnp.dot(hidden, w_down, preferred_element_type=jnp.float32))
    d_hidden = times_transpose(cotangent_rows, w_down)
    d_gate = (d_hidden * pre_up * sigmoid_gate * (1.0 + pre_gate * (1.0 - sigmoid_gate))).astype(
        jnp.bfloat16
    )
    d_up = (d_hidden * pre_gate * sigmoid_gate).astype(jnp.bfloat16)
    input_grad = scatter_y_first(times_transpose(d_gate, w_gate) + times_transpose(d_up, w_up))
    pseudo = jnp.sum(outer_frag[None] - every_local.astype(jnp.float32), axis=0)
    mean_delta = pseudo / every_local.shape[0]
    new_momentum = outer_beta * momentum + mean_delta
    new_outer = outer_frag - outer_rate * (mean_delta + outer_beta * new_momentum)
    return (layer_output, input_grad, new_outer, new_momentum)


def solution(mesh):
    in_specs = (
        P(AXES, None),
        P(AXES, None),
        P(None, "tensor"),
        P(None, "tensor"),
        P("tensor", None),
        P("tensor", None),
        P("replica", "tensor", None),
        P("tensor", None),
    )
    out_specs = (P(AXES, None), P(AXES, None), P("tensor", None), P("tensor", None))
    return jax.shard_map(
        on_device, mesh=mesh, in_specs=in_specs, out_specs=out_specs, check_vma=False
    )
```

```python
import jax
import jax.numpy as jnp
from jax import lax
from jax.experimental import pallas as pl
from jax.experimental.pallas import tpu as pltpu
from jax.sharding import PartitionSpec as P

outer_rate = 0.7
outer_beta = 0.9
AXES = ("replica", "tensor")
EXTENT_X, EXTENT_Y, EXTENT_Z = 4, 4, 4


def position(x, y, z, core):
    return ((y % 2) * EXTENT_X + x) * 16 + (y // 2) * 8 + z * 2 + core


def pairs(move):
    return [
        (position(x, y, z, core), position(*move(x, y, z, core)))
        for x in range(EXTENT_X)
        for y in range(EXTENT_Y)
        for z in range(EXTENT_Z)
        for core in range(2)
    ]


def send_z(rows, distance):
    return lax.ppermute(
        rows, AXES, pairs(lambda x, y, z, core: (x, y, (z + distance) % EXTENT_Z, core))
    )


def swap_y(rows):
    return lax.ppermute(rows, AXES, pairs(lambda x, y, z, core: (x, 3 - y, z, core)))


def swap_core(rows):
    return lax.ppermute(rows, AXES, pairs(lambda x, y, z, core: (x, y, z, 1 - core)))


def times_transpose(left_rows, weight):
    return lax.dot_general(
        left_rows, weight, (((1,), (1,)), ((), ())), preferred_element_type=jnp.float32
    )


def swap_x(rows, outer):
    def move(x, y, z, core):
        return (3 - x if outer else x ^ 1, y, z, core)

    return lax.ppermute(rows, AXES, pairs(move))


def swap_y_low(rows):
    return lax.ppermute(rows, AXES, pairs(lambda x, y, z, core: (x, y ^ 1, z, core)))


def order_z(block):
    one, three, two = send_z(block, -1), send_z(block, -3), send_z(block, -2)
    return [one, two, three]


def half(rows):
    return rows.astype(jnp.bfloat16)


def full(rows):
    return rows.astype(jnp.float32)


def sum_cores(partial):
    return partial[:128] + full(swap_core(half(partial[128:])))


def first_pseudo(outer_ref, here_ref, there_ref, sum_ref):
    outer = outer_ref[...]
    sum_ref[...] = (outer - full(here_ref[...])) + (outer - full(there_ref[...]))


def on_device(tokens, cotangent, w_gate, w_up, w_down, outer_frag, local_frag, momentum):
    width = tokens.shape[1]
    both = jnp.concatenate([tokens, swap_y(tokens)], 0)
    line = jnp.concatenate([cotangent] + order_z(cotangent), 0)
    local = local_frag[0]
    pseudo = pl.pallas_call(
        first_pseudo,
        out_shape=jax.ShapeDtypeStruct(outer_frag.shape, jnp.float32),
        cost_estimate=pl.CostEstimate(flops=25_000_000_000, bytes_accessed=0, transcendentals=0),
    )(outer_frag, local, swap_x(local, False))
    both, line, pseudo = lax.optimization_barrier((both, line, pseudo))
    token_near = jnp.concatenate([both] + order_z(both), 0)
    across = swap_y(line)
    pseudo = pseudo + swap_x(pseudo, True)
    cotangent_near = jnp.stack([line.reshape(4, 16, width), across.reshape(4, 16, width)], 1)
    cotangent_near = cotangent_near.reshape(128, width)
    token_rows = jnp.concatenate([token_near, swap_core(token_near)], 0)
    cotangent_rows = jnp.concatenate([cotangent_near, swap_core(cotangent_near)], 0)
    pre_gate = jnp.dot(token_rows, w_gate, preferred_element_type=jnp.float32)
    pre_up = jnp.dot(token_rows, w_up, preferred_element_type=jnp.float32)
    sigmoid_gate = jax.nn.sigmoid(pre_gate)
    hidden = (pre_gate * sigmoid_gate * pre_up).astype(jnp.bfloat16)
    hidden, pseudo = lax.optimization_barrier((hidden, pseudo))
    pseudo = pseudo + swap_y_low(pseudo)
    out_blocks = sum_cores(jnp.dot(hidden, w_down, preferred_element_type=jnp.float32))
    out_blocks = out_blocks.reshape(4, 32, width)
    out_sent = half(out_blocks[1:])
    d_hidden = times_transpose(cotangent_rows, w_down)
    d_gate = (d_hidden * pre_up * sigmoid_gate * (1.0 + pre_gate * (1.0 - sigmoid_gate))).astype(
        jnp.bfloat16
    )
    d_up = (d_hidden * pre_gate * sigmoid_gate).astype(jnp.bfloat16)
    out_sent, d_gate, d_up = lax.optimization_barrier((out_sent, d_gate, d_up))
    out_arrived = [send_z(out_sent[d - 1], d) for d in (1, 3, 2)]
    grad_blocks = sum_cores(times_transpose(d_gate, w_gate) + times_transpose(d_up, w_up))
    grad_blocks = grad_blocks.reshape(4, 2, 16, width)
    grad_line = grad_blocks[:, 0] + full(swap_y(half(grad_blocks[:, 1])))
    grad_sent = half(grad_line[1:])
    out_both = out_blocks[0] + full(out_arrived[0]) + full(out_arrived[1]) + full(out_arrived[2])
    layer_output = out_both[:16] + full(swap_y(half(out_both[16:])))
    grad_arrived = [send_z(grad_sent[d - 1], d) for d in (1, 3, 2)]
    input_grad = (
        grad_line[0] + full(grad_arrived[0]) + full(grad_arrived[1]) + full(grad_arrived[2])
    )
    mean_delta = pseudo / lax.axis_size("replica")
    new_momentum = outer_beta * momentum + mean_delta
    new_outer = outer_frag - outer_rate * (mean_delta + outer_beta * new_momentum)
    return (layer_output, input_grad, new_outer, new_momentum)


def solution(mesh):
    in_specs = (
        P(AXES, None),
        P(AXES, None),
        P(None, "tensor"),
        P(None, "tensor"),
        P("tensor", None),
        P("tensor", None),
        P("replica", "tensor", None),
        P("tensor", None),
    )
    out_specs = (P(AXES, None), P(AXES, None), P("tensor", None), P("tensor", None))
    return jax.shard_map(
        on_device, mesh=mesh, in_specs=in_specs, out_specs=out_specs, check_vma=False
    )
```

```python
import jax
import jax.numpy as jnp
from jax import lax
from jax.experimental import pallas as pl
from jax.experimental.pallas import tpu as pltpu
from jax.sharding import PartitionSpec as P

outer_rate = 0.7
outer_beta = 0.9
AXES = ("replica", "tensor")
EXTENT_X, EXTENT_Y, EXTENT_Z = 4, 4, 4
BF16, F32 = jnp.bfloat16, jnp.float32
MIB = 2**20
LONG, SHORT = 6.0, 0.004
ANY = pl.BlockSpec(memory_space=pl.ANY)
VMEM = pl.BlockSpec(memory_space=pltpu.VMEM)


def position(x, y, z, core):
    return ((y % 2) * EXTENT_X + x) * 16 + (y // 2) * 8 + z * 2 + core


def pairs(move):
    return [
        (position(x, y, z, core), position(*move(x, y, z, core)))
        for x in range(EXTENT_X)
        for y in range(EXTENT_Y)
        for z in range(EXTENT_Z)
        for core in range(2)
    ]


def send(rows, move):
    return lax.ppermute(rows, AXES, pairs(move))


def send_z(rows, distance):
    return send(rows, lambda x, y, z, core: (x, y, (z + distance) % EXTENT_Z, core))


def swap_y(rows):
    return send(rows, lambda x, y, z, core: (x, 3 - y, z, core))


def swap_core(rows):
    return send(rows, lambda x, y, z, core: (x, y, z, 1 - core))


def swap_x(rows, first):
    def move(x, y, z, core):
        return (x ^ 1 if (core == 0) == first else 3 - x, y, z, core)

    return send(rows, move)


def swap_y_low(rows):
    return send(rows, lambda x, y, z, core: (x, y ^ 1, z, core))


def half(rows):
    return rows.astype(BF16)


def full(rows):
    return rows.astype(F32)


def times(left, right):
    return jnp.dot(left, right, preferred_element_type=F32)


def times_transpose(left, right):
    return lax.dot_general(left, right, (((1,), (1,)), ((), ())), preferred_element_type=F32)


def cost(gflop):
    return pl.CostEstimate(flops=int(gflop * 1e9), bytes_accessed=0, transcendentals=0)


def load_weights(*refs):
    count = len(refs) // 2
    copies = [
        pltpu.make_async_copy(refs[i], refs[count + i], refs[-1].at[i]) for i in range(count)
    ]
    for copy in copies:
        copy.start()
    for copy in copies:
        copy.wait()


def weights_in_vmem(*weights):
    count = len(weights)
    return pl.pallas_call(
        load_weights,
        out_shape=[pltpu.VMEM(weight.shape, weight.dtype) for weight in weights],
        in_specs=[ANY] * count,
        out_specs=[ANY] * count,
        scratch_shapes=[pltpu.SemaphoreType.DMA((count,))],
        compiler_params=pltpu.CompilerParams(vmem_limit_bytes=MIB),
        cost_estimate=cost(LONG),
    )(*[pltpu.with_memory_space_constraint(weight, pltpu.HBM) for weight in weights])


def hidden_kernel(near_ref, far_ref, gate_ref, up_ref, hidden_ref, gate_factor_ref, up_factor_ref):
    rows = jnp.concatenate([near_ref[...], far_ref[...]], 0)
    for low in range(0, gate_ref.shape[1], 128):
        units = slice(low, low + 128)
        both = times(rows, jnp.concatenate([gate_ref[:, units], up_ref[:, units]], 1))
        pre_gate, pre_up = both[:, :128], both[:, 128:]
        sig = jax.nn.sigmoid(pre_gate)
        hidden_ref[:, units] = half(pre_gate * sig * pre_up)
        gate_factor_ref[:, units] = pre_up * sig * (1.0 + pre_gate * (1.0 - sig))
        up_factor_ref[:, units] = pre_gate * sig


def output_kernel(hidden_ref, down_ref, here_ref, there_ref):
    hidden = hidden_ref[...]
    for low in range(0, down_ref.shape[1], 512):
        features = slice(low, low + 512)
        partial = times(hidden, down_ref[:, features])
        here_ref[:, features] = partial[:128]
        there_ref[:, features] = half(partial[128:])


def d_hidden_kernel(near_ref, far_ref, down_ref, gate_factor_ref, up_factor_ref, grads_ref):
    rows = jnp.concatenate([near_ref[...], far_ref[...]], 0)
    count = down_ref.shape[0]
    for low in range(0, count, 256):
        high = min(low + 256, count)
        d_hidden = times_transpose(rows, down_ref[low:high, :])
        grads_ref[:, low:high] = half(d_hidden * gate_factor_ref[:, low:high])
        grads_ref[:, count + low : count + high] = half(d_hidden * up_factor_ref[:, low:high])


def grad_kernel(grads_ref, gate_ref, up_ref, here_ref, there_ref):
    grads = grads_ref[...]
    for low in range(0, gate_ref.shape[0], 256):
        features = slice(low, low + 256)
        weight = jnp.concatenate([gate_ref[features, :], up_ref[features, :]], 1)
        partial = times_transpose(grads, weight)
        here_ref[:, features] = partial[:128]
        there_ref[:, features] = half(partial[128:])


def sum_for_y_kernel(here_ref, far_ref, keep_ref, sent_ref):
    for d in range(4):
        kept, other, to = 32 * d, 32 * d + 16, slice(16 * d, 16 * d + 16)
        keep_ref[to, :] = here_ref[kept : kept + 16, :] + full(far_ref[kept : kept + 16, :])
        sent_ref[to, :] = half(here_ref[other : other + 16, :] + full(far_ref[other : other + 16, :]))


def sum_for_z_kernel(here_ref, far_ref, keep_ref, *sent_refs):
    keep_ref[...] = here_ref[:32, :] + full(far_ref[:32, :])
    for d, sent_ref in enumerate(sent_refs, 1):
        rows = slice(32 * d, 32 * d + 32)
        sent_ref[...] = half(here_ref[rows, :] + full(far_ref[rows, :]))


def line_kernel(here_ref, there_ref, line_ref, *sent_refs):
    line_ref[...] = here_ref[:16, :] + full(there_ref[:16, :])
    for d, sent_ref in enumerate(sent_refs, 1):
        rows = slice(16 * d, 16 * d + 16)
        sent_ref[...] = half(here_ref[rows, :] + full(there_ref[rows, :]))


def add_kernel(left_ref, right_ref, sum_ref):
    sum_ref[...] = left_ref[...] + right_ref[...]


def on_core(kernel, gflop, outs, *args, needs=()):
    def body(*refs):
        kernel(*refs[: len(args)], *refs[len(args) + len(needs) :])

    return pl.pallas_call(
        body,
        out_shape=[jax.ShapeDtypeStruct(shape, dtype) for shape, dtype in outs],
        in_specs=[VMEM] * len(args) + [ANY] * len(needs),
        out_specs=[VMEM] * len(outs),
        compiler_params=pltpu.CompilerParams(vmem_limit_bytes=12 * MIB),
        cost_estimate=cost(gflop),
    )(*args, *needs)


def tie(*values):
    return lax.optimization_barrier(values)


def place_own(tokens_hbm, cotangent_hbm, both_ref, line_ref, sems):
    moves = ((tokens_hbm, both_ref), (cotangent_hbm, line_ref))
    copies = [
        pltpu.make_async_copy(a, b.at[pl.ds(0, a.shape[0])], sems.at[i])
        for i, (a, b) in enumerate(moves)
    ]
    for copy in copies:
        copy.start()
    for copy in copies:
        copy.wait()


def own_rows_in_vmem(tokens, cotangent):
    rows, width = tokens.shape
    return pl.pallas_call(
        place_own,
        out_shape=[pltpu.VMEM((2 * rows, width), BF16), pltpu.VMEM((4 * rows, width), BF16)],
        in_specs=[ANY] * 2,
        out_specs=[ANY] * 2,
        scratch_shapes=[pltpu.SemaphoreType.DMA((2,))],
        compiler_params=pltpu.CompilerParams(vmem_limit_bytes=MIB),
        cost_estimate=cost(1.0),
    )(*[pltpu.with_memory_space_constraint(own, pltpu.HBM) for own in (tokens, cotangent)])


def after(value, *others):
    return tie(value, *others)[0]


def put(block, rows, at):
    return lax.dynamic_update_slice(block, rows, (at, 0))


def on_device(tokens, cotangent, w_gate, w_up, w_down, outer_frag, local_frag, momentum):
    width, units = w_gate.shape
    both, line = own_rows_in_vmem(tokens, cotangent)
    both = put(both, swap_y(tokens), 16)
    line_arrived = [send_z(cotangent, -d) for d in (1, 2, 3)]
    token_arrived = [send_z(both, -d) for d in (1, 2, 3)]
    (gate,) = weights_in_vmem(after(w_gate, both))
    line_arrived = tie(*line_arrived, gate)[:3]
    for d in (1, 2, 3):
        line = put(line, line_arrived[d - 1], 16 * d)
    across = swap_y(line)
    local = after(local_frag[0], gate)
    local_next = swap_y_low(local)
    up, down = weights_in_vmem(after(w_up, line), w_down)
    token_arrived = tie(*token_arrived, up, local_next)[:3]
    pseudo = (outer_frag - full(local)) + (outer_frag - full(local_next))
    token_near = jnp.concatenate([both] + list(token_arrived), 0)
    token_far = swap_core(token_near)
    hidden, gate_factor, up_factor = on_core(
        hidden_kernel,
        SHORT,
        [((256, units), BF16), ((256, units), F32), ((256, units), F32)],
        token_near,
        token_far,
        gate,
        up,
        needs=(pseudo,),
    )
    cotangent_near = jnp.stack([line.reshape(4, 16, width), across.reshape(4, 16, width)], 1)
    cotangent_near = cotangent_near.reshape(128, width)
    cotangent_far = swap_core(cotangent_near)
    pseudo_next = swap_x(pseudo, True)
    (grads,) = on_core(
        d_hidden_kernel,
        SHORT,
        [((256, 2 * units), BF16)],
        cotangent_near,
        cotangent_far,
        down,
        gate_factor,
        up_factor,
    )
    (pseudo,) = on_core(
        add_kernel, SHORT, [(pseudo.shape, F32)], pseudo, pseudo_next, needs=(grads,)
    )
    grad_here, grad_there = on_core(
        grad_kernel,
        LONG,
        [((128, width), F32), ((128, width), BF16)],
        grads,
        gate,
        up,
        needs=(pseudo,),
    )
    grad_far = swap_core(grad_there)
    out_here, out_there = on_core(
        output_kernel,
        SHORT,
        [((128, width), F32), ((128, width), BF16)],
        hidden,
        down,
        needs=(grad_there,),
    )
    out_far = swap_core(out_there)
    grad_keep, grad_sent = on_core(
        sum_for_y_kernel,
        SHORT,
        [((64, width), F32), ((64, width), BF16)],
        grad_here,
        grad_far,
        needs=(out_there,),
    )
    grad_across = swap_y(grad_sent)
    pseudo_next = swap_x(after(pseudo, out_there), False)
    out_keep, *out_sent = on_core(
        sum_for_z_kernel,
        SHORT,
        [((32, width), F32)] + [((32, width), BF16)] * 3,
        out_here,
        out_far,
        needs=(grad_sent,),
    )
    out_arrived = [send_z(out_sent[d - 1], d) for d in (1, 2, 3)]
    grad_line, *grad_sent = on_core(
        line_kernel,
        LONG,
        [((16, width), F32)] + [((16, width), BF16)] * 3,
        grad_keep,
        grad_across,
        needs=(out_sent[0],),
    )
    out_arrived = tie(*out_arrived, grad_sent[0])[:3]
    out_both = out_keep + full(out_arrived[0]) + full(out_arrived[1]) + full(out_arrived[2])
    out_sent = half(out_both[16:])
    layer_output = out_both[:16] + full(swap_y(out_sent))
    grad_arrived = [send_z(grad_sent[d - 1], d) for d in (1, 2, 3)]
    input_grad = (
        grad_line + full(grad_arrived[0]) + full(grad_arrived[1]) + full(grad_arrived[2])
    )
    (pseudo,) = on_core(
        add_kernel, SHORT, [(pseudo.shape, F32)], pseudo, pseudo_next, needs=(grad_line,)
    )
    mean_delta = pseudo / lax.axis_size("replica")
    new_momentum = outer_beta * momentum + mean_delta
    new_outer = outer_frag - outer_rate * (mean_delta + outer_beta * new_momentum)
    return (layer_output, input_grad, new_outer, new_momentum)


def solution(mesh):
    in_specs = (
        P(AXES, None),
        P(AXES, None),
        P(None, "tensor"),
        P(None, "tensor"),
        P("tensor", None),
        P("tensor", None),
        P("replica", "tensor", None),
        P("tensor", None),
    )
    out_specs = (P(AXES, None), P(AXES, None), P("tensor", None), P("tensor", None))
    return jax.shard_map(
        on_device, mesh=mesh, in_specs=in_specs, out_specs=out_specs, check_vma=False
    )
```

```python
import jax
import jax.numpy as jnp
from jax import lax
from jax.experimental import pallas as pl
from jax.experimental.pallas import tpu as pltpu
from jax.sharding import PartitionSpec as P

outer_rate = 0.7
outer_beta = 0.9
AXES = ("replica", "tensor")
EXTENT_X, EXTENT_Y, EXTENT_Z = 4, 4, 4
BF16, F32 = jnp.bfloat16, jnp.float32
MIB = 2**20
LONG, SHORT = 6.0, 0.004
ANY = pl.BlockSpec(memory_space=pl.ANY)
VMEM = pl.BlockSpec(memory_space=pltpu.VMEM)


def position(x, y, z, core):
    return ((y % 2) * EXTENT_X + x) * 16 + (y // 2) * 8 + z * 2 + core


def pairs(move):
    return [
        (position(x, y, z, core), position(*move(x, y, z, core)))
        for x in range(EXTENT_X)
        for y in range(EXTENT_Y)
        for z in range(EXTENT_Z)
        for core in range(2)
    ]


def send(rows, move):
    return lax.ppermute(rows, AXES, pairs(move))


def send_z(rows, distance):
    return send(rows, lambda x, y, z, core: (x, y, (z + distance) % EXTENT_Z, core))


def swap_y(rows):
    return send(rows, lambda x, y, z, core: (x, 3 - y, z, core))


def swap_core(rows):
    return send(rows, lambda x, y, z, core: (x, y, z, 1 - core))


def swap_x(rows, first):
    def move(x, y, z, core):
        return (x ^ 1 if (core == 0) == first else 3 - x, y, z, core)

    return send(rows, move)


def swap_y_low(rows):
    return send(rows, lambda x, y, z, core: (x, y ^ 1, z, core))


def half(rows):
    return rows.astype(BF16)


def full(rows):
    return rows.astype(F32)


def times(left, right):
    return jnp.dot(left, right, preferred_element_type=F32)


def times_transpose(left, right):
    return lax.dot_general(left, right, (((1,), (1,)), ((), ())), preferred_element_type=F32)


def cost(gflop):
    return pl.CostEstimate(flops=int(gflop * 1e9), bytes_accessed=0, transcendentals=0)


def load_weights(*refs):
    count = len(refs) // 2
    copies = [
        pltpu.make_async_copy(refs[i], refs[count + i], refs[-1].at[i]) for i in range(count)
    ]
    for copy in copies:
        copy.start()
    for copy in copies:
        copy.wait()


def weights_in_vmem(*weights):
    count = len(weights)
    return pl.pallas_call(
        load_weights,
        out_shape=[pltpu.VMEM(weight.shape, weight.dtype) for weight in weights],
        in_specs=[ANY] * count,
        out_specs=[ANY] * count,
        scratch_shapes=[pltpu.SemaphoreType.DMA((count,))],
        compiler_params=pltpu.CompilerParams(vmem_limit_bytes=MIB),
        cost_estimate=cost(LONG),
    )(*[pltpu.with_memory_space_constraint(weight, pltpu.HBM) for weight in weights])


def hidden_kernel(*refs):
    *piece_refs, gate_ref, up_ref, hidden_ref, gate_factor_ref, up_factor_ref = refs
    rows = jnp.concatenate([piece_ref[...] for piece_ref in piece_refs], 0)
    for low in range(0, gate_ref.shape[1], 128):
        units = slice(low, low + 128)
        both = times(rows, jnp.concatenate([gate_ref[:, units], up_ref[:, units]], 1))
        pre_gate, pre_up = both[:, :128], both[:, 128:]
        sig = jax.nn.sigmoid(pre_gate)
        hidden_ref[:, units] = half(pre_gate * sig * pre_up)
        gate_factor_ref[:, units] = pre_up * sig * (1.0 + pre_gate * (1.0 - sig))
        up_factor_ref[:, units] = pre_gate * sig


def output_kernel(hidden_ref, down_ref, here_ref, there_ref):
    hidden = hidden_ref[...]
    for low in range(0, down_ref.shape[1], 512):
        features = slice(low, low + 512)
        partial = times(hidden, down_ref[:, features])
        here_ref[:, features] = partial[:128]
        there_ref[:, features] = half(partial[128:])


def d_hidden_kernel(
    line_ref,
    across_ref,
    line_far_ref,
    across_far_ref,
    down_ref,
    gate_factor_ref,
    up_factor_ref,
    grads_ref,
):
    pieces = []
    for own_ref, other_ref in ((line_ref, across_ref), (line_far_ref, across_far_ref)):
        for d in range(4):
            pieces += [own_ref[16 * d : 16 * d + 16, :], other_ref[16 * d : 16 * d + 16, :]]
    rows = jnp.concatenate(pieces, 0)
    count = down_ref.shape[0]
    for low in range(0, count, 256):
        high = min(low + 256, count)
        d_hidden = times_transpose(rows, down_ref[low:high, :])
        grads_ref[:, low:high] = half(d_hidden * gate_factor_ref[:, low:high])
        grads_ref[:, count + low : count + high] = half(d_hidden * up_factor_ref[:, low:high])


def grad_kernel(grads_ref, gate_ref, up_ref, here_ref, there_ref):
    grads = grads_ref[...]
    for low in range(0, gate_ref.shape[0], 256):
        features = slice(low, low + 256)
        weight = jnp.concatenate([gate_ref[features, :], up_ref[features, :]], 1)
        partial = times_transpose(grads, weight)
        here_ref[:, features] = partial[:128]
        there_ref[:, features] = half(partial[128:])


def sum_for_y_kernel(here_ref, far_ref, keep_ref, sent_ref):
    for d in range(4):
        kept, other, to = 32 * d, 32 * d + 16, slice(16 * d, 16 * d + 16)
        keep_ref[to, :] = here_ref[kept : kept + 16, :] + full(far_ref[kept : kept + 16, :])
        sent_ref[to, :] = half(here_ref[other : other + 16, :] + full(far_ref[other : other + 16, :]))


def sum_for_z_kernel(here_ref, far_ref, keep_ref, *sent_refs):
    keep_ref[...] = here_ref[:32, :] + full(far_ref[:32, :])
    for d, sent_ref in enumerate(sent_refs, 1):
        rows = slice(32 * d, 32 * d + 32)
        sent_ref[...] = half(here_ref[rows, :] + full(far_ref[rows, :]))


def line_kernel(here_ref, there_ref, line_ref, *sent_refs):
    line_ref[...] = here_ref[:16, :] + full(there_ref[:16, :])
    for d, sent_ref in enumerate(sent_refs, 1):
        rows = slice(16 * d, 16 * d + 16)
        sent_ref[...] = half(here_ref[rows, :] + full(there_ref[rows, :]))


def both_kernel(here_ref, *refs):
    *arrived_refs, keep_ref, sent_ref = refs
    both = here_ref[...]
    for arrived_ref in arrived_refs:
        both += full(arrived_ref[...])
    keep_ref[...] = both[:16]
    sent_ref[...] = half(both[16:])


def add_kernel(left_ref, right_ref, sum_ref):
    sum_ref[...] = left_ref[...] + right_ref[...]


def on_core(kernel, gflop, outs, *args, needs=()):
    def body(*refs):
        kernel(*refs[: len(args)], *refs[len(args) + len(needs) :])

    return pl.pallas_call(
        body,
        out_shape=[jax.ShapeDtypeStruct(shape, dtype) for shape, dtype in outs],
        in_specs=[VMEM] * len(args) + [ANY] * len(needs),
        out_specs=[VMEM] * len(outs),
        compiler_params=pltpu.CompilerParams(vmem_limit_bytes=12 * MIB),
        cost_estimate=cost(gflop),
    )(*args, *needs)


def tie(*values):
    return lax.optimization_barrier(values)


def place_kernel(own_hbm, *refs):
    block_ref, sem = refs[-2:]
    copy = pltpu.make_async_copy(own_hbm, block_ref.at[pl.ds(0, own_hbm.shape[0])], sem)
    copy.start()
    copy.wait()


def place_own(own, times_rows, gflop, needs=()):
    rows, width = own.shape
    return pl.pallas_call(
        place_kernel,
        out_shape=[pltpu.VMEM((times_rows * rows, width), BF16)],
        in_specs=[ANY] * (1 + len(needs)),
        out_specs=[ANY],
        scratch_shapes=[pltpu.SemaphoreType.DMA],
        compiler_params=pltpu.CompilerParams(vmem_limit_bytes=MIB),
        cost_estimate=cost(gflop),
    )(pltpu.with_memory_space_constraint(own, pltpu.HBM), *needs)[0]


def after(value, *others):
    return tie(value, *others)[0]


def put(block, rows, at):
    return lax.dynamic_update_slice(block, rows, (at, 0))


def on_device(tokens, cotangent, w_gate, w_up, w_down, outer_frag, local_frag, momentum):
    width, units = w_gate.shape
    both = place_own(tokens, 2, 1.0)
    both = put(both, swap_y(tokens), 16)
    line_arrived = [send_z(cotangent, -d) for d in (1, 2, 3)]
    token_arrived = [send_z(both, -d) for d in (1, 2, 3)]
    line = place_own(cotangent, 4, LONG, needs=(both,))
    line_arrived = tie(*line_arrived, line)[:3]
    for d in (1, 2, 3):
        line = put(line, line_arrived[d - 1], 16 * d)
    across = swap_y(line)
    local = after(local_frag[0], line)
    local_next = swap_y_low(local)
    gate, up, down = weights_in_vmem(after(w_gate, line), w_up, w_down)
    token_arrived = tie(*token_arrived, up, local_next)[:3]
    pseudo = (outer_frag - full(local)) + (outer_frag - full(local_next))
    token_near = [both, *token_arrived]
    token_far = [swap_core(piece) for piece in token_near]
    hidden, gate_factor, up_factor = on_core(
        hidden_kernel,
        SHORT,
        [((256, units), BF16), ((256, units), F32), ((256, units), F32)],
        *token_near,
        *token_far,
        gate,
        up,
        needs=(across,),
    )
    line_far = swap_core(line)
    across_far = swap_core(after(across, hidden))
    out_here, out_there = on_core(
        output_kernel, SHORT, [((128, width), F32), ((128, width), BF16)], hidden, down
    )
    out_far = swap_core(out_there)
    pseudo_next = swap_x(pseudo, True)
    (pseudo,) = on_core(
        add_kernel, SHORT, [(pseudo.shape, F32)], pseudo, pseudo_next, needs=(out_there,)
    )
    (grads,) = on_core(
        d_hidden_kernel,
        LONG,
        [((256, 2 * units), BF16)],
        line,
        across,
        line_far,
        across_far,
        down,
        gate_factor,
        up_factor,
        needs=(out_there, pseudo),
    )
    out_keep, out_sent = on_core(
        sum_for_y_kernel,
        SHORT,
        [((64, width), F32), ((64, width), BF16)],
        out_here,
        out_far,
        needs=(grads,),
    )
    out_across = swap_y(out_sent)
    grad_here, grad_there = on_core(
        grad_kernel,
        LONG,
        [((128, width), F32), ((128, width), BF16)],
        grads,
        gate,
        up,
        needs=(out_sent,),
    )
    pseudo_next = swap_x(after(pseudo, grads), False)
    grad_keep, *grad_sent = on_core(
        sum_for_z_kernel,
        SHORT,
        [((32, width), F32)] + [((32, width), BF16)] * 3,
        grad_here,
        swap_core(grad_there),
    )
    grad_arrived = [send_z(grad_sent[d - 1], d) for d in (1, 2, 3)]
    (pseudo,) = on_core(
        add_kernel, SHORT, [(pseudo.shape, F32)], pseudo, pseudo_next, needs=(grad_sent[0],)
    )
    out_line, *out_sent = on_core(
        line_kernel,
        LONG,
        [((16, width), F32)] + [((16, width), BF16)] * 3,
        out_keep,
        out_across,
        needs=(grad_sent[0], pseudo),
    )
    grad_line, grad_sent = on_core(
        both_kernel,
        LONG,
        [((16, width), F32), ((16, width), BF16)],
        grad_keep,
        *grad_arrived,
    )
    input_grad = grad_line + full(swap_y(grad_sent))
    out_arrived = [send_z(out_sent[d - 1], d) for d in (1, 2, 3)]
    mean_delta = pseudo / lax.axis_size("replica")
    new_momentum = outer_beta * momentum + mean_delta
    new_outer = outer_frag - outer_rate * (mean_delta + outer_beta * new_momentum)
    out_arrived = tie(*out_arrived, grad_line)[:3]
    layer_output = out_line + full(out_arrived[0]) + full(out_arrived[1]) + full(out_arrived[2])
    return (layer_output, input_grad, new_outer, new_momentum)


def solution(mesh):
    in_specs = (
        P(AXES, None),
        P(AXES, None),
        P(None, "tensor"),
        P(None, "tensor"),
        P("tensor", None),
        P("tensor", None),
        P("replica", "tensor", None),
        P("tensor", None),
    )
    out_specs = (P(AXES, None), P(AXES, None), P("tensor", None), P("tensor", None))
    return jax.shard_map(
        on_device, mesh=mesh, in_specs=in_specs, out_specs=out_specs, check_vma=False
    )
```

```python
import jax
import jax.numpy as jnp
from jax import lax
from jax.experimental import pallas as pl
from jax.experimental.pallas import tpu as pltpu
from jax.sharding import PartitionSpec as P

outer_rate = 0.7
outer_beta = 0.9
AXES = ("replica", "tensor")
EXTENT_X, EXTENT_Y, EXTENT_Z = 4, 4, 4
BF16, F32 = jnp.bfloat16, jnp.float32
MIB = 2**20
LONG, SHORT = 6.0, 0.004
ANY = pl.BlockSpec(memory_space=pl.ANY)
VMEM = pl.BlockSpec(memory_space=pltpu.VMEM)


def position(x, y, z, core):
    return ((y % 2) * EXTENT_X + x) * 16 + (y // 2) * 8 + z * 2 + core


def pairs(move):
    return [
        (position(x, y, z, core), position(*move(x, y, z, core)))
        for x in range(EXTENT_X)
        for y in range(EXTENT_Y)
        for z in range(EXTENT_Z)
        for core in range(2)
    ]


def send(rows, move):
    return lax.ppermute(rows, AXES, pairs(move))


def send_z(rows, distance):
    return send(rows, lambda x, y, z, core: (x, y, (z + distance) % EXTENT_Z, core))


def swap_y(rows):
    return send(rows, lambda x, y, z, core: (x, 3 - y, z, core))


def swap_core(rows):
    return send(rows, lambda x, y, z, core: (x, y, z, 1 - core))


def swap_x(rows, first):
    def move(x, y, z, core):
        return (x ^ 1 if (core == 0) == first else 3 - x, y, z, core)

    return send(rows, move)


def swap_y_low(rows):
    return send(rows, lambda x, y, z, core: (x, y ^ 1, z, core))


def half(rows):
    return rows.astype(BF16)


def full(rows):
    return rows.astype(F32)


def times(left, right):
    return jnp.dot(left, right, preferred_element_type=F32)


def times_transpose(left, right):
    return lax.dot_general(left, right, (((1,), (1,)), ((), ())), preferred_element_type=F32)


def cost(gflop):
    return pl.CostEstimate(flops=int(gflop * 1e9), bytes_accessed=0, transcendentals=0)


def load_weights(*refs):
    count = len(refs) // 2
    copies = [
        pltpu.make_async_copy(refs[i], refs[count + i], refs[-1].at[i]) for i in range(count)
    ]
    for copy in copies:
        copy.start()
    for copy in copies:
        copy.wait()


def weights_in_vmem(*weights):
    count = len(weights)
    return pl.pallas_call(
        load_weights,
        out_shape=[pltpu.VMEM(weight.shape, weight.dtype) for weight in weights],
        in_specs=[ANY] * count,
        out_specs=[ANY] * count,
        scratch_shapes=[pltpu.SemaphoreType.DMA((count,))],
        compiler_params=pltpu.CompilerParams(vmem_limit_bytes=MIB),
        cost_estimate=cost(LONG),
    )(*[pltpu.with_memory_space_constraint(weight, pltpu.HBM) for weight in weights])


def hidden_kernel(*refs):
    *piece_refs, gate_ref, up_ref, hidden_ref, gate_factor_ref, up_factor_ref = refs
    rows = jnp.concatenate([piece_ref[...] for piece_ref in piece_refs], 0)
    for low in range(0, gate_ref.shape[1], 128):
        units = slice(low, low + 128)
        both = times(rows, jnp.concatenate([gate_ref[:, units], up_ref[:, units]], 1))
        pre_gate, pre_up = both[:, :128], both[:, 128:]
        sig = jax.nn.sigmoid(pre_gate)
        hidden_ref[:, units] = half(pre_gate * sig * pre_up)
        gate_factor_ref[:, units] = pre_up * sig * (1.0 + pre_gate * (1.0 - sig))
        up_factor_ref[:, units] = pre_gate * sig


def output_kernel(hidden_ref, down_ref, here_ref, there_ref):
    hidden = hidden_ref[...]
    for low in range(0, down_ref.shape[1], 512):
        features = slice(low, low + 512)
        partial = times(hidden, down_ref[:, features])
        here_ref[:, features] = partial[:128]
        there_ref[:, features] = half(partial[128:])


def d_hidden_kernel(
    line_ref,
    across_ref,
    line_far_ref,
    across_far_ref,
    down_ref,
    gate_factor_ref,
    up_factor_ref,
    grads_ref,
):
    pieces = []
    for own_ref, other_ref in ((line_ref, across_ref), (line_far_ref, across_far_ref)):
        for d in range(4):
            pieces += [own_ref[16 * d : 16 * d + 16, :], other_ref[16 * d : 16 * d + 16, :]]
    rows = jnp.concatenate(pieces, 0)
    count = down_ref.shape[0]
    for low in range(0, count, 256):
        high = min(low + 256, count)
        d_hidden = times_transpose(rows, down_ref[low:high, :])
        grads_ref[:, low:high] = half(d_hidden * gate_factor_ref[:, low:high])
        grads_ref[:, count + low : count + high] = half(d_hidden * up_factor_ref[:, low:high])


def grad_kernel(grads_ref, gate_ref, up_ref, here_ref, there_ref):
    grads = grads_ref[...]
    for low in range(0, gate_ref.shape[0], 256):
        features = slice(low, low + 256)
        weight = jnp.concatenate([gate_ref[features, :], up_ref[features, :]], 1)
        partial = times_transpose(grads, weight)
        here_ref[:, features] = partial[:128]
        there_ref[:, features] = half(partial[128:])


def sum_for_y_kernel(here_ref, far_ref, keep_ref, sent_ref):
    for d in range(4):
        kept, other, to = 32 * d, 32 * d + 16, slice(16 * d, 16 * d + 16)
        keep_ref[to, :] = here_ref[kept : kept + 16, :] + full(far_ref[kept : kept + 16, :])
        sent_ref[to, :] = half(here_ref[other : other + 16, :] + full(far_ref[other : other + 16, :]))


def sum_for_z_kernel(here_ref, far_ref, keep_ref, *sent_refs):
    keep_ref[...] = here_ref[:32, :] + full(far_ref[:32, :])
    for d, sent_ref in enumerate(sent_refs, 1):
        rows = slice(32 * d, 32 * d + 32)
        sent_ref[...] = half(here_ref[rows, :] + full(far_ref[rows, :]))


def line_kernel(here_ref, there_ref, line_ref, *sent_refs):
    line_ref[...] = here_ref[:16, :] + full(there_ref[:16, :])
    for d, sent_ref in enumerate(sent_refs, 1):
        rows = slice(16 * d, 16 * d + 16)
        sent_ref[...] = half(here_ref[rows, :] + full(there_ref[rows, :]))


def both_kernel(here_ref, *refs):
    *arrived_refs, keep_ref, sent_ref = refs
    both = here_ref[...]
    for arrived_ref in arrived_refs:
        both += full(arrived_ref[...])
    keep_ref[...] = both[:16]
    sent_ref[...] = half(both[16:])


def last_kernel(grad_line_ref, grad_across_ref, out_line_ref, *refs):
    *arrived_refs, output_ref, grad_ref = refs
    total = out_line_ref[...]
    for arrived_ref in arrived_refs:
        total += full(arrived_ref[...])
    output_ref[...] = total
    grad_ref[...] = grad_line_ref[...] + full(grad_across_ref[...])


def add_kernel(left_ref, right_ref, sum_ref):
    sum_ref[...] = left_ref[...] + right_ref[...]


def on_core(kernel, gflop, outs, *args, needs=()):
    def body(*refs):
        kernel(*refs[: len(args)], *refs[len(args) + len(needs) :])

    return pl.pallas_call(
        body,
        out_shape=[jax.ShapeDtypeStruct(shape, dtype) for shape, dtype in outs],
        in_specs=[VMEM] * len(args) + [ANY] * len(needs),
        out_specs=[VMEM] * len(outs),
        compiler_params=pltpu.CompilerParams(vmem_limit_bytes=12 * MIB),
        cost_estimate=cost(gflop),
    )(*args, *needs)


def tie(*values):
    return lax.optimization_barrier(values)


def place_kernel(tokens_hbm, cotangent_hbm, both_ref, line_ref, sems):
    moves = ((tokens_hbm, both_ref), (cotangent_hbm, line_ref))
    copies = [
        pltpu.make_async_copy(a, b.at[pl.ds(0, a.shape[0])], sems.at[i])
        for i, (a, b) in enumerate(moves)
    ]
    for copy in copies:
        copy.start()
    for copy in copies:
        copy.wait()


def place_own(tokens, cotangent):
    rows, width = tokens.shape
    return pl.pallas_call(
        place_kernel,
        out_shape=[pltpu.VMEM((2 * rows, width), BF16), pltpu.VMEM((4 * rows, width), BF16)],
        in_specs=[ANY] * 2,
        out_specs=[ANY] * 2,
        scratch_shapes=[pltpu.SemaphoreType.DMA((2,))],
        compiler_params=pltpu.CompilerParams(vmem_limit_bytes=MIB),
        cost_estimate=cost(1.0),
    )(*[pltpu.with_memory_space_constraint(own, pltpu.HBM) for own in (tokens, cotangent)])


def hold(block, *needs):
    return pl.pallas_call(
        lambda *refs: None,
        out_shape=pltpu.VMEM(block.shape, block.dtype),
        in_specs=[ANY] * (1 + len(needs)),
        out_specs=ANY,
        input_output_aliases={0: 0},
        compiler_params=pltpu.CompilerParams(vmem_limit_bytes=MIB),
        cost_estimate=cost(LONG),
    )(block, *needs)


def after(value, *others):
    return tie(value, *others)[0]


def put(block, rows, at):
    return lax.dynamic_update_slice(block, rows, (at, 0))


def on_device(tokens, cotangent, w_gate, w_up, w_down, outer_frag, local_frag, momentum):
    width, units = w_gate.shape
    both, line = place_own(tokens, cotangent)
    both = put(both, swap_y(tokens), 16)
    line_arrived = [send_z(cotangent, -d) for d in (1, 2, 3)]
    token_arrived = [send_z(both, -d) for d in (1, 2, 3)]
    line = hold(line, both)
    line_arrived = tie(*line_arrived, line)[:3]
    for d in (1, 2, 3):
        line = put(line, line_arrived[d - 1], 16 * d)
    across = swap_y(line)
    local = after(local_frag[0], line)
    local_next = swap_y_low(local)
    gate, up = weights_in_vmem(after(w_gate, line), w_up)
    down = pltpu.with_memory_space_constraint(w_down, pltpu.VMEM)
    token_arrived = tie(*token_arrived, up, local_next)[:3]
    pseudo = (outer_frag - full(local)) + (outer_frag - full(local_next))
    token_near = [both, *token_arrived]
    token_far = [swap_core(piece) for piece in token_near]
    hidden, gate_factor, up_factor = on_core(
        hidden_kernel,
        SHORT,
        [((256, units), BF16), ((256, units), F32), ((256, units), F32)],
        *token_near,
        *token_far,
        gate,
        up,
        needs=(across,),
    )
    line_far = swap_core(line)
    across_far = swap_core(after(across, hidden))
    out_here, out_there = on_core(
        output_kernel, SHORT, [((128, width), F32), ((128, width), BF16)], hidden, down
    )
    out_far = swap_core(out_there)
    pseudo_next = swap_x(pseudo, True)
    (pseudo,) = on_core(
        add_kernel, SHORT, [(pseudo.shape, F32)], pseudo, pseudo_next, needs=(out_there,)
    )
    (grads,) = on_core(
        d_hidden_kernel,
        LONG,
        [((256, 2 * units), BF16)],
        line,
        across,
        line_far,
        across_far,
        down,
        gate_factor,
        up_factor,
        needs=(out_there, pseudo),
    )
    out_keep, out_sent = on_core(
        sum_for_y_kernel,
        SHORT,
        [((64, width), F32), ((64, width), BF16)],
        out_here,
        out_far,
        needs=(grads,),
    )
    out_across = swap_y(out_sent)
    grad_here, grad_there = on_core(
        grad_kernel,
        LONG,
        [((128, width), F32), ((128, width), BF16)],
        grads,
        gate,
        up,
        needs=(out_sent,),
    )
    pseudo_next = swap_x(after(pseudo, grads), False)
    grad_keep, *grad_sent = on_core(
        sum_for_z_kernel,
        SHORT,
        [((32, width), F32)] + [((32, width), BF16)] * 3,
        grad_here,
        swap_core(grad_there),
    )
    grad_arrived = {d: send_z(grad_sent[d - 1], d) for d in (2, 1, 3)}
    grad_arrived = [grad_arrived[d] for d in (1, 2, 3)]
    (pseudo,) = on_core(
        add_kernel, SHORT, [(pseudo.shape, F32)], pseudo, pseudo_next, needs=(grad_sent[0],)
    )
    mean_delta = pseudo / lax.axis_size("replica")
    new_momentum = outer_beta * momentum + mean_delta
    new_outer = outer_frag - outer_rate * (mean_delta + outer_beta * new_momentum)
    out_line, *out_sent = on_core(
        line_kernel,
        LONG,
        [((16, width), F32)] + [((16, width), BF16)] * 3,
        out_keep,
        out_across,
        needs=(grad_sent[0], new_outer),
    )
    grad_line, grad_sent = on_core(
        both_kernel,
        LONG,
        [((16, width), F32), ((16, width), BF16)],
        grad_keep,
        grad_arrived[1],
        grad_arrived[0],
        grad_arrived[2],
    )
    out_arrived = [send_z(out_sent[d - 1], d) for d in (1, 2, 3)]
    layer_output, input_grad = on_core(
        last_kernel,
        SHORT,
        [((16, width), F32), ((16, width), F32)],
        grad_line,
        swap_y(grad_sent),
        out_line,
        *out_arrived,
    )
    return (layer_output, input_grad, new_outer, new_momentum)


def solution(mesh):
    in_specs = (
        P(AXES, None),
        P(AXES, None),
        P(None, "tensor"),
        P(None, "tensor"),
        P("tensor", None),
        P("tensor", None),
        P("replica", "tensor", None),
        P("tensor", None),
    )
    out_specs = (P(AXES, None), P(AXES, None), P("tensor", None), P("tensor", None))
    return jax.shard_map(
        on_device, mesh=mesh, in_specs=in_specs, out_specs=out_specs, check_vma=False
    )
```

```python
import jax
import jax.numpy as jnp
from jax import lax
from jax.experimental import pallas as pl
from jax.experimental.pallas import tpu as pltpu
from jax.sharding import PartitionSpec as P

outer_rate = 0.7
outer_beta = 0.9
AXES = ("replica", "tensor")
EXTENT_X, EXTENT_Y, EXTENT_Z = 4, 4, 4
BF16, F32 = jnp.bfloat16, jnp.float32
MIB = 2**20
LONG, SHORT = 6.0, 0.004
ANY = pl.BlockSpec(memory_space=pl.ANY)
VMEM = pl.BlockSpec(memory_space=pltpu.VMEM)


def position(x, y, z, core):
    return ((y % 2) * EXTENT_X + x) * 16 + (y // 2) * 8 + z * 2 + core


def pairs(move):
    return [
        (position(x, y, z, core), position(*move(x, y, z, core)))
        for x in range(EXTENT_X)
        for y in range(EXTENT_Y)
        for z in range(EXTENT_Z)
        for core in range(2)
    ]


def send(rows, move):
    return lax.ppermute(rows, AXES, pairs(move))


def send_z(rows, distance):
    return send(rows, lambda x, y, z, core: (x, y, (z + distance) % EXTENT_Z, core))


def swap_y(rows):
    return send(rows, lambda x, y, z, core: (x, 3 - y, z, core))


def swap_core(rows):
    return send(rows, lambda x, y, z, core: (x, y, z, 1 - core))


def swap_x(rows, first):
    def move(x, y, z, core):
        return (x ^ 1 if (core == 0) == first else 3 - x, y, z, core)

    return send(rows, move)


def swap_y_low(rows):
    return send(rows, lambda x, y, z, core: (x, y ^ 1, z, core))


def half(rows):
    return rows.astype(BF16)


def full(rows):
    return rows.astype(F32)


def times(left, right):
    return jnp.dot(left, right, preferred_element_type=F32)


def times_transpose(left, right):
    return lax.dot_general(left, right, (((1,), (1,)), ((), ())), preferred_element_type=F32)


def cost(gflop):
    return pl.CostEstimate(flops=int(gflop * 1e9), bytes_accessed=0, transcendentals=0)


def load_weights(*refs):
    count = len(refs) // 2
    copies = [
        pltpu.make_async_copy(refs[i], refs[count + i], refs[-1].at[i]) for i in range(count)
    ]
    for copy in copies:
        copy.start()
    for copy in copies:
        copy.wait()


def weights_in_vmem(*weights):
    count = len(weights)
    return pl.pallas_call(
        load_weights,
        out_shape=[pltpu.VMEM(weight.shape, weight.dtype) for weight in weights],
        in_specs=[ANY] * count,
        out_specs=[ANY] * count,
        scratch_shapes=[pltpu.SemaphoreType.DMA((count,))],
        compiler_params=pltpu.CompilerParams(vmem_limit_bytes=MIB),
        cost_estimate=cost(LONG),
    )(*[pltpu.with_memory_space_constraint(weight, pltpu.HBM) for weight in weights])


def hidden_kernel(*refs):
    *piece_refs, gate_ref, up_ref, hidden_ref, gate_factor_ref, up_factor_ref = refs
    rows = jnp.concatenate([piece_ref[...] for piece_ref in piece_refs], 0)
    for low in range(0, gate_ref.shape[1], 128):
        units = slice(low, low + 128)
        both = times(rows, jnp.concatenate([gate_ref[:, units], up_ref[:, units]], 1))
        pre_gate, pre_up = both[:, :128], both[:, 128:]
        sig = jax.nn.sigmoid(pre_gate)
        hidden_ref[:, units] = half(pre_gate * sig * pre_up)
        gate_factor_ref[:, units] = pre_up * sig * (1.0 + pre_gate * (1.0 - sig))
        up_factor_ref[:, units] = pre_gate * sig


def output_kernel(hidden_ref, down_ref, here_ref, there_ref):
    hidden = hidden_ref[...]
    for low in range(0, down_ref.shape[1], 512):
        features = slice(low, low + 512)
        partial = times(hidden, down_ref[:, features])
        here_ref[:, features] = partial[:128]
        there_ref[:, features] = half(partial[128:])


def d_hidden_kernel(
    line_ref,
    across_ref,
    line_far_ref,
    across_far_ref,
    down_ref,
    gate_factor_ref,
    up_factor_ref,
    grads_ref,
):
    pieces = []
    for own_ref, other_ref in ((line_ref, across_ref), (line_far_ref, across_far_ref)):
        for d in range(4):
            pieces += [own_ref[16 * d : 16 * d + 16, :], other_ref[16 * d : 16 * d + 16, :]]
    rows = jnp.concatenate(pieces, 0)
    count = down_ref.shape[0]
    for low in range(0, count, 256):
        high = min(low + 256, count)
        d_hidden = times_transpose(rows, down_ref[low:high, :])
        grads_ref[:, low:high] = half(d_hidden * gate_factor_ref[:, low:high])
        grads_ref[:, count + low : count + high] = half(d_hidden * up_factor_ref[:, low:high])


def grad_kernel(grads_ref, gate_ref, up_ref, here_ref, there_ref):
    grads = grads_ref[...]
    for low in range(0, gate_ref.shape[0], 256):
        features = slice(low, low + 256)
        weight = jnp.concatenate([gate_ref[features, :], up_ref[features, :]], 1)
        partial = times_transpose(grads, weight)
        here_ref[:, features] = partial[:128]
        there_ref[:, features] = half(partial[128:])


def sum_for_y_kernel(here_ref, far_ref, keep_ref, sent_ref):
    for d in range(4):
        kept, other, to = 32 * d, 32 * d + 16, slice(16 * d, 16 * d + 16)
        keep_ref[to, :] = here_ref[kept : kept + 16, :] + full(far_ref[kept : kept + 16, :])
        sent_ref[to, :] = half(here_ref[other : other + 16, :] + full(far_ref[other : other + 16, :]))


def sum_for_z_kernel(here_ref, far_ref, keep_ref, *sent_refs):
    keep_ref[...] = here_ref[:32, :] + full(far_ref[:32, :])
    for d, sent_ref in enumerate(sent_refs, 1):
        rows = slice(32 * d, 32 * d + 32)
        sent_ref[...] = half(here_ref[rows, :] + full(far_ref[rows, :]))


def line_kernel(here_ref, there_ref, line_ref, *sent_refs):
    line_ref[...] = here_ref[:16, :] + full(there_ref[:16, :])
    for d, sent_ref in enumerate(sent_refs, 1):
        rows = slice(16 * d, 16 * d + 16)
        sent_ref[...] = half(here_ref[rows, :] + full(there_ref[rows, :]))


def both_kernel(here_ref, *refs):
    *arrived_refs, keep_ref, sent_ref = refs
    both = here_ref[...]
    for arrived_ref in arrived_refs:
        both += full(arrived_ref[...])
    keep_ref[...] = both[:16]
    sent_ref[...] = half(both[16:])


def last_kernel(grad_line_ref, grad_across_ref, out_line_ref, *refs):
    *arrived_refs, output_ref, grad_ref = refs
    total = out_line_ref[...]
    for arrived_ref in arrived_refs:
        total += full(arrived_ref[...])
    output_ref[...] = total
    grad_ref[...] = grad_line_ref[...] + full(grad_across_ref[...])


def add_kernel(left_ref, right_ref, sum_ref):
    sum_ref[...] = left_ref[...] + right_ref[...]


def on_core(kernel, gflop, outs, *args, needs=()):
    def body(*refs):
        kernel(*refs[: len(args)], *refs[len(args) + len(needs) :])

    return pl.pallas_call(
        body,
        out_shape=[jax.ShapeDtypeStruct(shape, dtype) for shape, dtype in outs],
        in_specs=[VMEM] * len(args) + [ANY] * len(needs),
        out_specs=[VMEM] * len(outs),
        compiler_params=pltpu.CompilerParams(vmem_limit_bytes=12 * MIB),
        cost_estimate=cost(gflop),
    )(*args, *needs)


def tie(*values):
    return lax.optimization_barrier(values)


def place_kernel(tokens_hbm, cotangent_hbm, both_ref, line_ref, sems):
    moves = ((tokens_hbm, both_ref), (cotangent_hbm, line_ref))
    copies = [
        pltpu.make_async_copy(a, b.at[pl.ds(0, a.shape[0])], sems.at[i])
        for i, (a, b) in enumerate(moves)
    ]
    for copy in copies:
        copy.start()
    for copy in copies:
        copy.wait()


def place_own(tokens, cotangent):
    rows, width = tokens.shape
    return pl.pallas_call(
        place_kernel,
        out_shape=[pltpu.VMEM((2 * rows, width), BF16), pltpu.VMEM((4 * rows, width), BF16)],
        in_specs=[ANY] * 2,
        out_specs=[ANY] * 2,
        scratch_shapes=[pltpu.SemaphoreType.DMA((2,))],
        compiler_params=pltpu.CompilerParams(vmem_limit_bytes=MIB),
        cost_estimate=cost(1.0),
    )(*[pltpu.with_memory_space_constraint(own, pltpu.HBM) for own in (tokens, cotangent)])


def hold(block, *needs):
    return pl.pallas_call(
        lambda *refs: None,
        out_shape=pltpu.VMEM(block.shape, block.dtype),
        in_specs=[ANY] * (1 + len(needs)),
        out_specs=ANY,
        input_output_aliases={0: 0},
        compiler_params=pltpu.CompilerParams(vmem_limit_bytes=MIB),
        cost_estimate=cost(LONG),
    )(block, *needs)


def after(value, *others):
    return tie(value, *others)[0]


def put(block, rows, at):
    return lax.dynamic_update_slice(block, rows, (at, 0))


def on_device(tokens, cotangent, w_gate, w_up, w_down, outer_frag, local_frag, momentum):
    width, units = w_gate.shape
    both, line = place_own(tokens, cotangent)
    both = put(both, swap_y(tokens), 16)
    line_arrived = [send_z(cotangent, -d) for d in (1, 2, 3)]
    token_arrived = [send_z(both, -d) for d in (1, 2, 3)]
    line = hold(line, both)
    line_arrived = tie(*line_arrived, line)[:3]
    for d in (1, 2, 3):
        line = put(line, line_arrived[d - 1], 16 * d)
    across = swap_y(line)
    local = after(local_frag[0], line)
    local_next = swap_y_low(local)
    (gate,) = weights_in_vmem(after(w_gate, line))
    up, down = [
        pltpu.with_memory_space_constraint(weight, pltpu.VMEM) for weight in (w_up, w_down)
    ]
    token_arrived = tie(*token_arrived, gate, local_next)[:3]
    pseudo = (outer_frag - full(local)) + (outer_frag - full(local_next))
    token_near = [both, *token_arrived]
    token_far = [swap_core(piece) for piece in token_near]
    hidden, gate_factor, up_factor = on_core(
        hidden_kernel,
        SHORT,
        [((256, units), BF16), ((256, units), F32), ((256, units), F32)],
        *token_near,
        *token_far,
        gate,
        up,
        needs=(across,),
    )
    line_far = swap_core(line)
    across_far = swap_core(after(across, hidden))
    out_here, out_there = on_core(
        output_kernel, SHORT, [((128, width), F32), ((128, width), BF16)], hidden, down
    )
    out_far = swap_core(out_there)
    pseudo_next = swap_x(pseudo, True)
    (pseudo,) = on_core(
        add_kernel, SHORT, [(pseudo.shape, F32)], pseudo, pseudo_next, needs=(out_there,)
    )
    (grads,) = on_core(
        d_hidden_kernel,
        LONG,
        [((256, 2 * units), BF16)],
        line,
        across,
        line_far,
        across_far,
        down,
        gate_factor,
        up_factor,
        needs=(out_there, pseudo),
    )
    out_keep, out_sent = on_core(
        sum_for_y_kernel,
        SHORT,
        [((64, width), F32), ((64, width), BF16)],
        out_here,
        out_far,
        needs=(grads,),
    )
    out_across = swap_y(out_sent)
    grad_here, grad_there = on_core(
        grad_kernel,
        SHORT,
        [((128, width), F32), ((128, width), BF16)],
        grads,
        gate,
        up,
        needs=(out_sent,),
    )
    pseudo_next = swap_x(after(pseudo, grads), False)
    grad_keep, *grad_sent = on_core(
        sum_for_z_kernel,
        SHORT,
        [((32, width), F32)] + [((32, width), BF16)] * 3,
        grad_here,
        swap_core(grad_there),
    )
    grad_arrived = {d: send_z(grad_sent[d - 1], d) for d in (2, 1, 3)}
    grad_arrived = [grad_arrived[d] for d in (1, 2, 3)]
    (pseudo,) = on_core(
        add_kernel, SHORT, [(pseudo.shape, F32)], pseudo, pseudo_next, needs=(grad_sent[0],)
    )
    mean_delta = pseudo / lax.axis_size("replica")
    new_momentum = outer_beta * momentum + mean_delta
    new_outer = outer_frag - outer_rate * (mean_delta + outer_beta * new_momentum)
    out_line, *out_sent = on_core(
        line_kernel,
        SHORT,
        [((16, width), F32)] + [((16, width), BF16)] * 3,
        out_keep,
        out_across,
        needs=(grad_sent[0], new_outer),
    )
    grad_line, grad_sent = on_core(
        both_kernel,
        LONG,
        [((16, width), F32), ((16, width), BF16)],
        grad_keep,
        grad_arrived[1],
        grad_arrived[0],
        grad_arrived[2],
    )
    out_arrived = [send_z(out_sent[d - 1], d) for d in (1, 2, 3)]
    layer_output, input_grad = on_core(
        last_kernel,
        SHORT,
        [((16, width), F32), ((16, width), F32)],
        grad_line,
        swap_y(grad_sent),
        out_line,
        *out_arrived,
    )
    return (layer_output, input_grad, new_outer, new_momentum)


def solution(mesh):
    in_specs = (
        P(AXES, None),
        P(AXES, None),
        P(None, "tensor"),
        P(None, "tensor"),
        P("tensor", None),
        P("tensor", None),
        P("replica", "tensor", None),
        P("tensor", None),
    )
    out_specs = (P(AXES, None), P(AXES, None), P("tensor", None), P("tensor", None))
    return jax.shard_map(
        on_device, mesh=mesh, in_specs=in_specs, out_specs=out_specs, check_vma=False
    )
```
